512 devices in a mesh: gx: 16 (over z), gy: 32 (over x, y, core).
Axes of the slice: x: 4, y: 4, z: 16, core: 2. Of those that a mesh axis runs over, the one named last changes fastest.
Arguments:
- state: bfloat16 [2, 16, 512, 4096], P(None, None, 'gx', 'gy'), may hold values from -6 to 6
- potential: float32 [512, 4096], P('gx', 'gy'), may hold values from -1 to 1
- bonds: int32 [2, 512, 4096], P(None, 'gx', 'gy'), may hold values 0 or 1
- coeffs: float32 [4], replicated, may hold values from 0.3 to 0.9
- boundary: int32 [1], replicated, may hold values from 1024 to 3071
- counting: float32 [1], replicated, may hold values from 0.5 to 2.5
Outputs:
- evolved: bfloat16 [2, 16, 512, 4096], P(None, None, 'gx', 'gy')
- intersection: float32 [2, 16, 16], replicated
The draws below stay inside these ranges and needn't reach their ends.
All inputs are finite; a program needn't handle non-finite values. No bound on the sum of `bonds` on one device may be relied on, other than what follows from the above.
Results may differ from the reference program's by a relative error of at most 0.0013.
Values sent between devices are 32-bit elements; how exact they have to be, the bound alone decides.
No kernel may reach another device: no remote copies, remote signals or barrier semaphores. Data moves between devices by JAX's collectives and lax.ppermute only.
A program may use at most 64 MiB of HBM per device.

```python
import jax
import jax.numpy as jnp
from jax import lax

NORB = 16
KTERMS = 4
STEPS = 3
NX = 512
NY = 4096


def with_ends(values, own_key, low, top_value):
    longest = values.shape.index(max(values.shape))
    spots = []
    for shift in (0, 1):
        where = [jax.random.randint(jax.random.fold_in(own_key, axis), (), 0, length) for axis, length in enumerate(values.shape)]
        where[longest] = (where[longest] + shift) % values.shape[longest]
        spots.append(tuple(where))
    return values.at[spots[0]].set(low).at[spots[1]].set(top_value)


def steps_of(own_key, extent, cuts, least, high):
    def one(axis_at, parts):
        draws = jax.random.uniform(jax.random.fold_in(jax.random.fold_in(own_key, 6), axis_at), (parts,), jnp.float32, least / len(cuts), high / len(cuts))
        return jnp.repeat(jnp.exp(draws), extent[axis_at] // parts).reshape((-1,) + (1,) * (len(extent) - axis_at - 1))

    loudness = one(*cuts[0])
    for cut in cuts[1:]:
        loudness = loudness * one(*cut)
    return loudness


def bell_draw(stream_key, extent, width, bound, cuts=(), kind=jnp.bfloat16):
    factor_of = steps_of(stream_key, extent, cuts, -0.22, 0.18) if cuts else 1.0
    values = jax.random.normal(stream_key, extent, jnp.float32) * width * factor_of
    return jnp.minimum(jnp.maximum(values, -bound), bound).astype(kind)


def setup_inputs(seed: int = 0) -> dict:
    arg_keys = jax.random.split(jax.random.key(seed), 7)
    return {
        "state": bell_draw(arg_keys[0], (2, NORB, NX, NY), 1.0, 6.0, ((2, 16), (3, 32))),
        "potential": jnp.clip(jax.random.uniform(arg_keys[1], (NX, NY), jnp.float32, -1.0, 1.0) * steps_of(arg_keys[1], (NX, NY), ((0, 16), (1, 32)), -0.4, 0.0), -1.0, 1.0),
        "bonds": with_ends((jax.random.randint(arg_keys[2], (2, NX, NY), 0, 8) < 7).astype(jnp.int32), jax.random.fold_in(arg_keys[2], 1), 0, 1),
        "coeffs": jnp.clip(jax.random.uniform(arg_keys[3], (KTERMS,), jnp.float32, 0.3, 0.9), 0.3, 0.9),
        "boundary": jax.random.randint(arg_keys[4], (1,), NY // 4, 3 * NY // 4).astype(jnp.int32),
        "counting": jnp.clip(jax.random.uniform(arg_keys[5], (1,), jnp.float32, 0.5, 2.5), 0.5, 2.5),
    }


energy_scale = 5.0


def hamilton(wave, potential, mask_row, mask_col):
    zero_row = jnp.zeros_like(wave[:, :1, :])
    zero_col = jnp.zeros_like(wave[:, :, :1])
    below = jnp.concatenate([wave[:, 1:, :], zero_row], axis=1)
    moved_row = mask_row * wave
    above = jnp.concatenate([zero_row, moved_row[:, :-1, :]], axis=1)
    right_side = jnp.concatenate([wave[:, :, 1:], zero_col], axis=2)
    moved_col = mask_col * wave
    left_side = jnp.concatenate([zero_col, moved_col[:, :, :-1]], axis=2)
    hopping = mask_row * below + above + mask_col * right_side + left_side
    return (potential * wave - hopping) / energy_scale


def evolve_one(wave, potential, mask_row, mask_col, coeffs):
    current = wave.astype(jnp.float32)
    for repeat in range(STEPS):
        term_zero = current
        term_one = hamilton(term_zero, potential, mask_row, mask_col)
        term_two = 2.0 * hamilton(term_one, potential, mask_row, mask_col) - term_zero
        term_three = 2.0 * hamilton(term_two, potential, mask_row, mask_col) - term_one
        real_part = coeffs[0] * term_zero[0] + coeffs[1] * term_one[1] - coeffs[2] * term_two[0] - coeffs[3] * term_three[1]
        imag_part = coeffs[0] * term_zero[1] - coeffs[1] * term_one[0] - coeffs[2] * term_two[1] + coeffs[3] * term_three[0]
        current = jnp.stack([real_part, imag_part])
    return current.astype(jnp.bfloat16)


def reference(state, potential, bonds, coeffs, boundary, counting):
    mask_row = bonds[0].astype(jnp.float32)
    mask_col = bonds[1].astype(jnp.float32)
    orbitals = jnp.transpose(state, (1, 0, 2, 3))
    evolved = lax.map(lambda wave: evolve_one(wave, potential, mask_row, mask_col, coeffs), orbitals)
    evolved = jnp.transpose(evolved, (1, 0, 2, 3))
    flat = evolved.reshape(2, NORB, NX * NY)
    columns = jnp.tile(jnp.arange(NY, dtype=jnp.int32), NX)
    inside = (columns >= boundary[0]).astype(jnp.bfloat16)
    real_amp, imag_amp = flat[0], flat[1]
    real_right, imag_right = real_amp * inside, imag_amp * inside
    total_re = jnp.dot(real_amp, real_amp.T, preferred_element_type=jnp.float32) + jnp.dot(imag_amp, imag_amp.T, preferred_element_type=jnp.float32)
    total_im = jnp.dot(real_amp, imag_amp.T, preferred_element_type=jnp.float32) - jnp.dot(imag_amp, real_amp.T, preferred_element_type=jnp.float32)
    right_re = jnp.dot(real_amp, real_right.T, preferred_element_type=jnp.float32) + jnp.dot(imag_amp, imag_right.T, preferred_element_type=jnp.float32)
    right_im = jnp.dot(real_amp, imag_right.T, preferred_element_type=jnp.float32) - jnp.dot(imag_amp, real_right.T, preferred_element_type=jnp.float32)
    cosine = jnp.cos(counting[0]) - 1.0
    sine = jnp.sin(counting[0])
    count = float(NX * NY)
    over_re = (total_re + cosine * right_re - sine * right_im) / count
    over_im = (total_im + cosine * right_im + sine * right_re) / count
    return evolved, jnp.stack([over_re, over_im])
```

```python
import jax
import jax.numpy as jnp
from jax import lax
from jax.experimental import pallas as pl
from jax.experimental.pallas import tpu as pltpu
from jax.sharding import PartitionSpec as P

STEPS = 3
DEPTH = 3 * STEPS
ROWS, COLS, FIELDS = 32, 128, 32
GROUPS = 4
SPAN = COLS // GROUPS
TALL = ROWS + 2 * DEPTH
TALL_PAD = 56
TILE = 8 * (GROUPS + 1)
THIRD = 17
ROW_MSG = DEPTH * FIELDS + 3 * 16
COL_MSG = 8 * THIRD + TALL_PAD

f32 = jnp.float32


def lanes_of(shape):
    return lax.broadcasted_iota(jnp.int32, shape, len(shape) - 1)


def pack_rows(state, potential, bonds, wave, masks, to_prev, to_next):
    last_x = lax.axis_index("gx") == lax.axis_size("gx") - 1
    last_y = lax.axis_index("gy") == lax.axis_size("gy") - 1
    for f in range(FIELDS):
        own = state[f].astype(f32)
        wave[pl.ds(f, ROWS, stride=FIELDS), :] = pltpu.roll(own, SPAN * (f // 8), 1) if f >= 8 else own
    row = lax.broadcasted_iota(jnp.int32, (ROWS, COLS), 0)
    lane = lanes_of((ROWS, COLS))
    masks[0] = potential[...]
    masks[1] = jnp.where(jnp.logical_and(last_x, row == ROWS - 1), 0.0, bonds[0].astype(f32))
    masks[2] = jnp.where(jnp.logical_and(last_y, lane == COLS - 1), 0.0, bonds[1].astype(f32))
    many = DEPTH * FIELDS
    to_prev[:many] = wave[:many]
    to_next[:many] = wave[ROWS * FIELDS - many :]
    for m in range(3):
        to_prev[many + 16 * m : many + 16 * m + 16] = masks[m, :16]
        to_next[many + 16 * m : many + 16 * m + 16] = masks[m, ROWS - 16 :]


def pack_columns(wave, masks, above, below, rotated, to_left, to_right):
    many = DEPTH * FIELDS
    lane = lanes_of((8, COLS))
    inner = lane % SPAN
    block = lane // SPAN

    def merged(parts, first):
        out = parts[first % GROUPS]
        for b in range(1, GROUPS):
            out = jnp.where(block[:1] == b, parts[(b + first) % GROUPS], out)
        return out

    def packed_left(a, b, c):
        return jnp.where(inner[:1] < 9, a, jnp.where(inner[:1] < 18, pltpu.roll(b, 9, 1), pltpu.roll(c, 18, 1)))

    def packed_right(a, b, c):
        back = lambda v, by: pltpu.roll(v, COLS - by, 1)
        return jnp.where(inner[:1] >= SPAN - 9, a, jnp.where(inner[:1] >= SPAN - 18, back(b, 9), back(c, 18)))

    lefts, rights = [], []
    for i in range(TALL):
        if i < DEPTH:
            ref, at = above, i * FIELDS
        elif i < DEPTH + ROWS:
            ref, at = wave, (i - DEPTH) * FIELDS
        else:
            ref, at = below, (i - DEPTH - ROWS) * FIELDS
        parts = [ref[at + 8 * k : at + 8 * k + 8] for k in range(GROUPS)]
        lefts.append(merged(parts, 0))
        rights.append(merged(parts, 1))
    lefts.append(lefts[0])
    rights.append(rights[0])
    for t in range(THIRD):
        to_left[8 * t : 8 * t + 8] = packed_left(lefts[t], lefts[t + THIRD], lefts[t + 2 * THIRD])
        to_right[8 * t : 8 * t + 8] = packed_right(rights[t], rights[t + THIRD], rights[t + 2 * THIRD])
    left_masks, right_masks = [], []
    for m in range(3):
        at = many + 16 * m
        tall = jnp.concatenate(
            [
                above[at + 16 - DEPTH : at + 16],
                masks[m],
                below[at : at + DEPTH],
                jnp.zeros((TALL_PAD - TALL, COLS), f32),
            ],
            axis=0,
        )
        parts = [pltpu.roll(tall, SPAN * k, 1) if k else tall for k in range(GROUPS)]
        for k in range(GROUPS):
            rotated[m, k] = parts[k]
        left_masks.append(merged(parts, 0))
        right_masks.append(merged(parts, 1))
    to_left[8 * THIRD :] = packed_left(*left_masks)
    to_right[8 * THIRD :] = packed_right(*right_masks)


def evolve(
    coeffs, boundary, phase, wave, above, below, rotated, from_right, from_left, evolved, shares,
    cur, one, two, spread, halo_masks, flat, cells,
):
    lane = lanes_of((8, COLS))
    near = (lane % SPAN) < SPAN // 2
    near_row = near[:1]

    def joined(right, left, u):
        if u:
            right = pltpu.roll(right, COLS - 9 * u, 1)
            left = pltpu.roll(left, 9 * u, 1)
        return jnp.where(near_row, right, left)

    for i in range(TALL):
        if i < DEPTH:
            ref, at = above, i * FIELDS
        elif i < DEPTH + ROWS:
            ref, at = wave, (i - DEPTH) * FIELDS
        else:
            ref, at = below, (i - DEPTH - ROWS) * FIELDS
        cur[TILE * i : TILE * i + FIELDS] = ref[at : at + FIELDS]
        t, u = i % THIRD, i // THIRD
        cur[TILE * i + FIELDS : TILE * i + TILE] = joined(
            from_right[8 * t : 8 * t + 8], from_left[8 * t : 8 * t + 8], u
        )
    for m in range(3):
        halo_masks[m] = joined(from_right[8 * THIRD :], from_left[8 * THIRD :], m)
        for i in range(TALL):
            for k in range(GROUPS):
                spread[m, TILE * i + 8 * k : TILE * i + 8 * k + 8] = jnp.broadcast_to(rotated[m, k, i : i + 1], (8, COLS))
            spread[m, TILE * i + FIELDS : TILE * i + TILE] = jnp.broadcast_to(halo_masks[m, i : i + 1], (8, COLS))

    lane_main = lanes_of((FIELDS, COLS))
    group_main = lax.broadcasted_iota(jnp.int32, (FIELDS, COLS), 0) // 8
    seam_left = lane_main == SPAN * group_main
    seam_right = lane_main == (SPAN * group_main + COLS - 1) % COLS
    left_at = [lane == SPAN * k for k in range(GROUPS)]
    right_at = [lane == (SPAN * k + COLS - 1) % COLS for k in range(GROUPS)]

    def sewn(shifted, seam, at):
        main, rim = shifted[:FIELDS], shifted[FIELDS:]
        over = jnp.where(seam, jnp.concatenate([rim] * GROUPS, axis=0), main)
        for k in range(GROUPS):
            rim = jnp.where(at[k], main[8 * k : 8 * k + 8], rim)
        return jnp.concatenate([over, rim], axis=0)

    def row_of(ref, i):
        return ref[TILE * i : TILE * i + TILE]

    def hamilton(source, first, after, finish):
        here = row_of(source, first)
        handed = row_of(spread.at[1], first - 1) * row_of(source, first - 1)
        for i in range(first, after):
            following = row_of(source, i + 1)
            pot, down, side = (row_of(spread.at[m], i) for m in range(3))
            right = sewn(pltpu.roll(here, COLS - 1, 1), seam_right, right_at)
            left = sewn(pltpu.roll(side * here, 1, 1), seam_left, left_at)
            hop = (down * following + handed) + (side * right + left)
            finish(i, pot * here - hop)
            handed = down * here
            here = following

    c0, c1, c2, c3 = (coeffs[k] for k in range(4))
    e3 = 4.0 * c3 / 125.0
    scale = e3 * e3 * e3
    one_vec = jnp.ones((1, COLS), f32)
    per = 1.0 / (one_vec * e3)
    a0 = one_vec * (c0 + c2) * per
    a1 = one_vec * ((c1 + 3.0 * c3) / 5.0) * per
    a2 = one_vec * (2.0 * c2 / 25.0) * per

    def put(ref, i, value):
        ref[TILE * i : TILE * i + TILE] = value

    def second(i, value):
        start = row_of(cur, i)
        put(two, i, a1 * start - value)
        put(cur, i, a0 * start - a2 * value)

    half = FIELDS // 2
    real_lanes = (lane + SPAN // 2) % COLS < COLS // 2

    def third(i, value):
        turned = pltpu.roll(value, COLS // 2, 1)
        start = row_of(cur, i)
        re = start[:half] + turned[half:FIELDS]
        im = start[half:FIELDS] - turned[:half]
        rim = start[FIELDS:] + jnp.where(real_lanes, turned[FIELDS:], -turned[FIELDS:])
        put(cur, i, jnp.concatenate([re, im, rim], axis=0))

    for step in range(STEPS):
        d = 3 * step
        hamilton(cur, d + 1, TALL - d - 1, lambda i, value: put(one, i, value))
        hamilton(one, d + 2, TALL - d - 2, second)
        hamilton(two, d + 3, TALL - d - 3, third)

    for r in range(ROWS):
        at = TILE * (r + DEPTH)
        for k in range(GROUPS):
            part = cur[at + 8 * k : at + 8 * k + 8] * scale
            if k:
                part = pltpu.roll(part, COLS - SPAN * k, 1)
            cells[r * FIELDS + 8 * k : r * FIELDS + 8 * k + 8] = part
        flat[:, COLS * r : COLS * r + COLS] = cells[r * FIELDS : r * FIELDS + FIELDS].astype(jnp.bfloat16)
    for f in range(FIELDS):
        evolved[f] = cells[pl.ds(f, ROWS, stride=FIELDS), :].astype(jnp.bfloat16)

    first_col = lax.axis_index("gy") * COLS
    inside = (lanes_of((1, COLS)) + first_col >= boundary[0]).astype(f32).astype(jnp.bfloat16)
    amps = flat[...]
    amps_right = jnp.concatenate([amps[:, COLS * r : COLS * r + COLS] * inside for r in range(ROWS)], axis=1)
    contract = (((1,), (1,)), ((), ()))
    total = lax.dot_general(amps, amps, contract, preferred_element_type=f32)
    right = lax.dot_general(amps, amps_right, contract, preferred_element_type=f32)
    n = half
    total_re = total[:n, :n] + total[n:, n:]
    total_im = total[:n, n:] - total[n:, :n]
    right_re = right[:n, :n] + right[n:, n:]
    right_im = right[:n, n:] - right[n:, :n]
    cosine, sine, count = phase[0], phase[1], phase[2]
    over_re = (total_re + cosine * right_re - sine * right_im) * count
    over_im = (total_im + cosine * right_im + sine * right_re) * count
    wide = jnp.concatenate([over_re, over_im], axis=0)
    tile = jnp.concatenate([wide[8 * k : 8 * k + 8] for k in range(4)] + [jnp.zeros((8, COLS - 4 * n), f32)], axis=1)
    for p in range(shares.shape[0]):
        shares[p] = tile


def add_and_copy(parts, shares):
    total = jnp.sum(parts[...], axis=0)
    for p in range(shares.shape[0]):
        shares[p] = total


def add_and_open(parts, out):
    total = jnp.sum(parts[...], axis=0)
    n = out.shape[-1]
    for k in range(4):
        out[k // 2, 8 * (k % 2) : 8 * (k % 2) + 8] = total[:, n * k : n * k + n]


def whole():
    return pl.BlockSpec(memory_space=pltpu.VMEM)


def scalars():
    return pl.BlockSpec(memory_space=pltpu.SMEM)


def call(kernel, outs, in_specs, scratch=(), limit=None):
    return pl.pallas_call(
        kernel,
        out_shape=[jax.ShapeDtypeStruct(s, d) for s, d in outs],
        in_specs=in_specs,
        out_specs=[whole()] * len(outs),
        scratch_shapes=list(scratch),
        compiler_params=pltpu.CompilerParams(vmem_limit_bytes=limit) if limit else None,
    )


def moved(array, axis, by):
    peers = lax.axis_size(axis)
    return lax.ppermute(array, axis, [(i, (i + by) % peers) for i in range(peers)])


def on_device(state, potential, bonds, coeffs, boundary, counting):
    norbit = state.shape[1]
    peers_x, peers_y = lax.axis_size("gx"), lax.axis_size("gy")
    count = float(ROWS * COLS * peers_x * peers_y)
    phase = jnp.stack([jnp.cos(counting[0]) - 1.0, jnp.sin(counting[0]), jnp.float32(1.0 / count)])
    wave, masks, to_prev, to_next = call(
        pack_rows,
        [((ROWS * FIELDS, COLS), f32), ((3, ROWS, COLS), f32), ((ROW_MSG, COLS), f32), ((ROW_MSG, COLS), f32)],
        [whole()] * 3,
    )(state.reshape(FIELDS, ROWS, COLS), potential, bonds)
    above = moved(to_next, "gx", 1)
    below = moved(to_prev, "gx", -1)
    rotated, to_left, to_right = call(
        pack_columns,
        [((3, GROUPS, TALL_PAD, COLS), f32), ((COL_MSG, COLS), f32), ((COL_MSG, COLS), f32)],
        [whole()] * 4,
    )(wave, masks, above, below)
    from_right = moved(to_left, "gy", -1)
    from_left = moved(to_right, "gy", 1)
    evolved, shares = call(
        evolve,
        [((FIELDS, ROWS, COLS), jnp.bfloat16), ((peers_y, 8, COLS), f32)],
        [scalars()] * 3 + [whole()] * 6,
        [
            pltpu.VMEM((TILE * TALL, COLS), f32),
            pltpu.VMEM((TILE * TALL, COLS), f32),
            pltpu.VMEM((TILE * TALL, COLS), f32),
            pltpu.VMEM((3, TILE * TALL, COLS), f32),
            pltpu.VMEM((3, TALL_PAD, COLS), f32),
            pltpu.VMEM((FIELDS, ROWS * COLS), jnp.bfloat16),
            pltpu.VMEM((ROWS * FIELDS, COLS), f32),
        ],
        limit=40 * 1024 * 1024,
    )(coeffs, boundary, phase, wave, above, below, rotated, from_right, from_left)
    parts = lax.all_to_all(shares, "gy", 0, 0, tiled=True)
    (shares,) = call(add_and_copy, [((peers_x, 8, COLS), f32)], [whole()])(parts)
    parts = lax.all_to_all(shares, "gx", 0, 0, tiled=True)
    (over,) = call(add_and_open, [((2, norbit, norbit), f32)], [whole()])(parts)
    return evolved.reshape(state.shape), over


def solution(mesh):
    return jax.shard_map(
        on_device,
        mesh=mesh,
        in_specs=(P(None, None, "gx", "gy"), P("gx", "gy"), P(None, "gx", "gy"), P(), P(), P()),
        out_specs=(P(None, None, "gx", "gy"), P()),
        check_vma=False,
    )
```

```python
import jax
import jax.numpy as jnp
from jax import lax
from jax.experimental import pallas as pl
from jax.experimental.pallas import tpu as pltpu
from jax.sharding import PartitionSpec as P

STEPS = 3
DEPTH = 3 * STEPS
ROWS, COLS, FIELDS = 32, 128, 32
GROUPS = 4
HALF = COLS // 2
TALL = ROWS + 2 * DEPTH
TALL_PAD = 56
BATCH = 16
CHUNK = 8
PIECES = 7
PLACES = 8
EDGE = DEPTH * FIELDS
THIN = 16
ROW_MSG = EDGE + 3 * 16
COL_MSG = THIN * PLACES + TALL_PAD
MIB = 1024 * 1024

f32 = jnp.float32


def lanes():
    return lax.broadcasted_iota(jnp.int32, (1, COLS), 1)


def inner_lanes():
    return lanes() & (HALF - 1)


def turn(value, by):
    by = by % COLS
    return pltpu.roll(value, by, value.ndim - 1) if by else value


def ends(a, b):
    low = lanes() < HALF
    return jnp.where(low, a, turn(b, HALF)), jnp.where(low, turn(a, HALF), b)


def own_strip(head, tail):
    return jnp.where(inner_lanes() < HALF // 2, turn(head, DEPTH), turn(tail, -DEPTH))


def packed(parts, first):
    out = turn(parts[0], -first)
    for u in range(1, len(parts)):
        out = jnp.where(inner_lanes() < DEPTH * u, out, turn(parts[u], DEPTH * u - first))
    return out


def join(from_left, own, from_right, u):
    inner = inner_lanes()
    left = turn(from_left, -DEPTH * u)
    right = turn(from_right, HALF - DEPTH - DEPTH * u)
    return jnp.where(inner < DEPTH, left, jnp.where(inner < HALF - DEPTH, own, right))


def ends_of(ref, at):
    groups = [ref[at + 8 * g : at + 8 * g + 8] for g in range(GROUPS)]
    both = [ends(groups[2 * p], groups[2 * p + 1]) for p in range(2)]
    return tuple(jnp.concatenate([pair[k] for pair in both], axis=0) for k in range(2))


def fetched(sources, targets, sems):
    copies = [pltpu.make_async_copy(s, t, sems.at[k]) for k, (s, t) in enumerate(zip(sources, targets))]
    for copy in copies:
        copy.start()
    for copy in copies:
        copy.wait()


def bond_masks(bonds, rows):
    last_x = lax.axis_index("gx") == lax.axis_size("gx") - 1
    last_y = lax.axis_index("gy") == lax.axis_size("gy") - 1
    down, side = (bonds[m, rows].astype(f32) for m in range(2))
    row = lax.broadcasted_iota(jnp.int32, down.shape, 0) + rows.start
    down = jnp.where(jnp.logical_and(last_x, row == ROWS - 1), 0.0, down)
    side = jnp.where(jnp.logical_and(last_y, lanes() == COLS - 1), 0.0, side)
    return down, side


def pack_rows(state_at, potential_at, bonds_at, to_prev, to_next, state, potential, bonds, sems):
    fetched((state_at, potential_at, bonds_at), (state, potential, bonds), sems)
    for ref, rows, skip in ((to_prev, slice(0, 16), 0), (to_next, slice(16, 32), 16 - DEPTH)):
        for f in range(FIELDS):
            part = state[f, rows].astype(f32)[skip : skip + DEPTH]
            ref[pl.ds(f, 8, stride=FIELDS), :] = part[:8]
            ref[8 * FIELDS + f : 8 * FIELDS + f + 1] = part[8:]
        down, side = bond_masks(bonds, rows)
        for m, value in enumerate((potential[rows], down, side)):
            ref[EDGE + 16 * m : EDGE + 16 * m + 16] = value


def turn_bulk(state_at, potential_at, bonds_at, wave, masks, heads, tails, state, potential, bonds, sems):
    fetched((state_at, potential_at, bonds_at), (state, potential, bonds), sems)
    for f in range(FIELDS):
        wave[pl.ds(f, ROWS, stride=FIELDS), :] = state[f].astype(f32)
    down, side = bond_masks(bonds, slice(0, ROWS))
    for m, value in enumerate((potential[...], down, side)):
        masks[m] = value
    for i in range(ROWS):
        rows = slice(THIN * i, THIN * i + THIN)
        heads[rows], tails[rows] = ends_of(wave, FIELDS * i)


def tall_mask(masks, above, below, m):
    at = EDGE + 16 * m
    pad = jnp.zeros((TALL_PAD - TALL, COLS), f32)
    return jnp.concatenate([above[at + 16 - DEPTH : at + 16], masks[m], below[at : at + DEPTH], pad], axis=0)


def row_ends(above, below, heads, tails):
    both = []
    for i in range(TALL):
        if DEPTH <= i < DEPTH + ROWS:
            rows = slice(THIN * (i - DEPTH), THIN * (i - DEPTH) + THIN)
            both.append((heads[rows], tails[rows]))
        else:
            ref, at = (above, i) if i < DEPTH else (below, i - DEPTH - ROWS)
            both.append(ends_of(ref, FIELDS * at))
    return both


def pack_columns(above, below, masks, heads, tails, on_chip, off_chip, own, own_masks):
    even = lax.axis_index("gy") % 2 == 0

    def send(rows, heads, tails):
        head, tail = packed(heads, 0), packed(tails, HALF - DEPTH)
        on_chip[rows] = jnp.where(even, tail, head)
        off_chip[rows] = jnp.where(even, head, tail)

    both = row_ends(above, below, heads, tails)
    for t in range(PLACES):
        parts = both[t::PLACES]
        send(slice(THIN * t, THIN * t + THIN), [p[0] for p in parts], [p[1] for p in parts])
    parts = []
    for m in range(3):
        mask = tall_mask(masks, above, below, m)
        parts.append(ends(mask, mask))
        own_masks[m] = own_strip(*parts[m])
    send(slice(THIN * PLACES, COL_MSG), [p[0] for p in parts], [p[1] for p in parts])
    for i in range(TALL):
        own[THIN * i : THIN * i + THIN] = own_strip(*both[i])


def spread_rows(spread, m, value, count=TALL):
    for i in range(count):
        spread[m, 8 * i : 8 * i + 8] = jnp.broadcast_to(value[i : i + 1], (8, COLS))


def hamilton(source, masks, wide, first, after, finish):
    many = BATCH if wide == THIN else 1

    def rows_of(i, some):
        return source[wide * i : wide * (i + some)].reshape(some, wide, COLS)

    def mask_of(m, i, some):
        one = masks[m, 8 * i : 8 * (i + some)].reshape(some, 8, COLS)
        return jnp.concatenate([one] * (wide // 8), axis=1)

    for i in range(first, after, many):
        some = min(many, after - i)
        here = rows_of(i, some)
        pot, down, side = (mask_of(m, i, some) for m in range(3))
        right = turn(here, -1)
        left = turn(side * here, 1)
        handed = mask_of(1, i - 1, some) * rows_of(i - 1, some)
        hop = (down * rows_of(i + 1, some) + handed) + (side * right + left)
        finish(slice(wide * i, wide * (i + some)), pot * here - hop)


def factors(coeffs):
    c0, c1, c2, c3 = (coeffs[k] for k in range(4))
    one = jnp.ones((1, COLS), f32)
    e3 = 4.0 * c3 / 125.0
    per = 1.0 / (one * e3)
    return one * (c0 + c2) * per, one * ((c1 + 3.0 * c3) / 5.0) * per, one * (2.0 * c2 / 25.0) * per, e3


def step_of(start, out, one, two, masks, wide, d, weights):
    a0, a1, a2, _ = weights

    half = wide // 2

    def put(ref, rows, value):
        ref[rows] = value.reshape(-1, COLS)

    def get(ref, rows):
        return ref[rows].reshape(-1, wide, COLS)

    def first(rows, value):
        put(one, rows, value)

    def second(rows, value):
        x = get(start, rows)
        put(two, rows, a1 * x - value)
        put(out, rows, a0 * x - a2 * value)

    def third(rows, value):
        kept = get(out, rows)
        parts = [kept[:, :half] + value[:, half:], kept[:, half:] - value[:, :half]]
        put(out, rows, jnp.concatenate(parts, axis=1))

    hamilton(start, masks, wide, d + 1, TALL - d - 1, first)
    hamilton(one, masks, wide, d + 2, TALL - d - 2, second)
    hamilton(two, masks, wide, d + 3, TALL - d - 3, third)


def evolve_main(coeffs, wave, above, below, masks, main, spread, cur, one, two):
    for m in range(3):
        spread_rows(spread, m, tall_mask(masks, above, below, m))
    cur[:EDGE] = above[:EDGE]
    cur[EDGE : EDGE + ROWS * FIELDS] = wave[...]
    cur[EDGE + ROWS * FIELDS :] = below[:EDGE]
    weights = factors(coeffs)
    for step in range(STEPS):
        step_of(cur, cur, one, two, spread, FIELDS, 3 * step, weights)
    main[...] = cur[EDGE : EDGE + ROWS * FIELDS]


def evolve_rest(
    coeffs, boundary, phase, main, own, own_masks, on_chip, off_chip, evolved, part, strip, one, two, spread, cells, flat
):
    even = lax.axis_index("gy") % 2 == 0

    def received(rows):
        a, b = on_chip[rows], off_chip[rows]
        return jnp.where(even, b, a), jnp.where(even, a, b)

    left, right = received(slice(THIN * PLACES, COL_MSG))
    for m in range(3):
        spread_rows(spread, m, join(left, own_masks[m], right, m))
    for t in range(PLACES):
        left, right = received(slice(THIN * t, THIN * t + THIN))
        for u in range(PIECES):
            i = t + u * PLACES
            if i < TALL:
                rows = slice(THIN * i, THIN * i + THIN)
                strip[rows] = join(left, own[rows], right, u)

    weights = factors(coeffs)
    for step in range(STEPS):
        step_of(strip, strip, one, two, spread, THIN, 3 * step, weights)

    e3 = weights[3]
    scale = e3 * e3 * e3
    for r in range(0, ROWS, CHUNK):
        rim = strip[THIN * (r + DEPTH) : THIN * (r + DEPTH + CHUNK)].reshape(CHUNK, THIN, COLS)
        rows = slice(FIELDS * r, FIELDS * (r + CHUNK))
        middle = main[rows].reshape(CHUNK, FIELDS, COLS)
        parts = []
        for g in range(GROUPS):
            mine, by = rim[:, 8 * (g // 2) : 8 * (g // 2) + 8], HALF * (g % 2)
            value = jnp.where(lanes() < DEPTH, turn(mine, -by - DEPTH), middle[:, 8 * g : 8 * g + 8])
            parts.append(jnp.where(lanes() >= COLS - DEPTH, turn(mine, HALF + DEPTH - by), value))
        done = jnp.concatenate(parts, axis=1) * scale
        cells[rows] = done.reshape(CHUNK * FIELDS, COLS)
        for k in range(CHUNK):
            flat[:, COLS * (r + k) : COLS * (r + k + 1)] = done[k].astype(jnp.bfloat16)
    for f in range(FIELDS):
        evolved[f] = cells[pl.ds(f, ROWS, stride=FIELDS), :].astype(jnp.bfloat16)

    first_col = lax.axis_index("gy") * COLS
    inside = (lanes() + first_col >= boundary[0]).astype(f32).astype(jnp.bfloat16)
    amps = flat[...]
    amps_right = jnp.concatenate([amps[:, COLS * r : COLS * r + COLS] * inside for r in range(ROWS)], axis=1)
    contract = (((1,), (1,)), ((), ()))
    total = lax.dot_general(amps, amps, contract, preferred_element_type=f32)
    right = lax.dot_general(amps, amps_right, contract, preferred_element_type=f32)
    n = FIELDS // 2
    total_re = total[:n, :n] + total[n:, n:]
    total_im = total[:n, n:] - total[n:, :n]
    right_re = right[:n, :n] + right[n:, n:]
    right_im = right[:n, n:] - right[n:, :n]
    cosine, sine, count = phase[0], phase[1], phase[2]
    over_re = (total_re + cosine * right_re - sine * right_im) * count
    over_im = (total_im + cosine * right_im + sine * right_re) * count
    wide = jnp.concatenate([over_re, over_im], axis=0)
    tiles = [wide[8 * g : 8 * g + 8] for g in range(GROUPS)] + [jnp.zeros((8, COLS - GROUPS * n), f32)]
    tile = jnp.concatenate(tiles, axis=1)
    for p in range(part.shape[0]):
        part[p] = tile


def call(kernel, outs, inputs, scalars=0, fetch=False, scratch=(), limit=8, flops=100_000):
    moved = sum(4 * x.size for x in inputs)
    shapes = [pltpu.VMEM(s, d) for s, d in scratch]
    if fetch:
        shapes += [pltpu.VMEM(x.shape, x.dtype) for x in inputs] + [pltpu.SemaphoreType.DMA((len(inputs),))]
    space = pltpu.HBM if fetch else pltpu.VMEM
    return pl.pallas_call(
        kernel,
        out_shape=[jax.ShapeDtypeStruct(s, d) for s, d in outs],
        in_specs=[pl.BlockSpec(memory_space=pltpu.SMEM if k < scalars else space) for k in range(len(inputs))],
        out_specs=[pl.BlockSpec(memory_space=pltpu.VMEM)] * len(outs),
        scratch_shapes=shapes,
        compiler_params=pltpu.CompilerParams(vmem_limit_bytes=limit * MIB),
        cost_estimate=pl.CostEstimate(flops=flops, bytes_accessed=moved, transcendentals=0),
    )(*inputs)


def added(parts, axis):
    return jnp.sum(lax.all_to_all(parts, axis, 0, 0, tiled=True), axis=0)


def on_device(state, potential, bonds, coeffs, boundary, counting):
    norbit = state.shape[1]
    peers_x, peers_y = lax.axis_size("gx"), lax.axis_size("gy")
    count = float(ROWS * COLS * peers_x * peers_y)
    phase = jnp.stack([jnp.cos(counting[0]) - 1.0, jnp.sin(counting[0]), jnp.float32(1.0 / count)])
    fields = state.reshape(FIELDS, ROWS, COLS)

    to_prev, to_next = call(pack_rows, [((ROW_MSG, COLS), f32)] * 2, (fields, potential, bonds), fetch=True)
    above = lax.ppermute(to_next, "gx", [(i, (i + 1) % peers_x) for i in range(peers_x)])
    below = lax.ppermute(to_prev, "gx", [(i, (i - 1) % peers_x) for i in range(peers_x)])
    thin_own = ((THIN * ROWS, COLS), f32)
    wave, masks, heads, tails = call(
        turn_bulk,
        [((ROWS * FIELDS, COLS), f32), ((3, ROWS, COLS), f32), thin_own, thin_own],
        (fields, potential, bonds),
        fetch=True,
    )
    tall, thin, spread = ((FIELDS * TALL, COLS), f32), ((THIN * TALL, COLS), f32), ((3, 8 * TALL, COLS), f32)
    on_chip, off_chip, own, own_masks = call(
        pack_columns,
        [((COL_MSG, COLS), f32), ((COL_MSG, COLS), f32), thin, ((3, TALL_PAD, COLS), f32)],
        (above, below, masks, heads, tails),
    )
    on_chip = lax.ppermute(on_chip, "gy", [(i, i ^ 1) for i in range(peers_y)])
    off_chip = lax.ppermute(off_chip, "gy", [(i, (i + 2 * (i % 2) - 1) % peers_y) for i in range(peers_y)])
    (main,) = call(
        evolve_main,
        [((FIELDS * ROWS, COLS), f32)],
        (coeffs, wave, above, below, masks),
        scalars=1,
        scratch=[spread] + [tall] * 3,
        limit=12,
        flops=20_000_000,
    )
    evolved, part = call(
        evolve_rest,
        [((FIELDS, ROWS, COLS), jnp.bfloat16), ((peers_y, 8, COLS), f32)],
        (coeffs, boundary, phase, main, own, own_masks, on_chip, off_chip),
        scalars=3,
        scratch=[thin] * 3 + [spread, ((FIELDS * ROWS, COLS), f32), ((FIELDS, ROWS * COLS), jnp.bfloat16)],
        limit=12,
        flops=10_000_000,
    )
    total = added(part, "gy")
    total = added(jnp.broadcast_to(total[None], (peers_x,) + total.shape), "gx")
    over = total[:, : GROUPS * norbit].reshape(8, GROUPS, norbit).transpose(1, 0, 2).reshape(2, norbit, norbit)
    return evolved.reshape(state.shape), over


def solution(mesh):
    return jax.shard_map(
        on_device,
        mesh=mesh,
        in_specs=(P(None, None, "gx", "gy"), P("gx", "gy"), P(None, "gx", "gy"), P(), P(), P()),
        out_specs=(P(None, None, "gx", "gy"), P()),
        check_vma=False,
    )
```

```python
import jax
import jax.numpy as jnp
from jax import lax
from jax.experimental import pallas as pl
from jax.experimental.pallas import tpu as pltpu
from jax.sharding import PartitionSpec as P

STEPS = 3
DEPTH = 3 * STEPS
ROWS, COLS, FIELDS = 32, 128, 32
GROUPS = 4
HALF = COLS // 2
TALL = ROWS + 2 * DEPTH
TALL_PAD = 64
QUARTER = TALL_PAD // 4
BATCH = 16
CHUNK = 8
PIECES = 7
OWN_PLACES, PLACES = 5, 8
EDGE = DEPTH * FIELDS
THIN = 16
ROW_MSG = EDGE + 3 * 16
COL_MSG = THIN * PLACES + QUARTER
MORE = 8
MIB = 1024 * 1024
FIRST_LIMIT = 62

f32 = jnp.float32


def lanes():
    return lax.broadcasted_iota(jnp.int32, (1, COLS), 1)


def inner_lanes():
    return lanes() & (HALF - 1)


def turn(value, by):
    by = by % COLS
    return pltpu.roll(value, by, value.ndim - 1) if by else value


def ends(a, b):
    low = lanes() < HALF
    return jnp.where(low, a, turn(b, HALF)), jnp.where(low, turn(a, HALF), b)


def own_strip(head, tail):
    return jnp.where(inner_lanes() < HALF // 2, turn(head, DEPTH), turn(tail, -DEPTH))


def packed(parts, first):
    out = turn(parts[0], -first)
    for u in range(1, len(parts)):
        out = jnp.where(inner_lanes() < DEPTH * u, out, turn(parts[u], DEPTH * u - first))
    return out


def join(from_left, own, from_right, u):
    inner = inner_lanes()
    left = turn(from_left, -DEPTH * u)
    right = turn(from_right, HALF - DEPTH - DEPTH * u)
    return jnp.where(inner < DEPTH, left, jnp.where(inner < HALF - DEPTH, own, right))


def ends_of(ref, at):
    groups = [ref[at + 8 * g : at + 8 * g + 8] for g in range(GROUPS)]
    both = [ends(groups[2 * p], groups[2 * p + 1]) for p in range(2)]
    return tuple(jnp.concatenate([pair[k] for pair in both], axis=0) for k in range(2))


def pack_places(both, first, heads, tails):
    for t in range(0, len(both), PIECES):
        rows = slice(THIN * (first + t // PIECES), THIN * (first + t // PIECES) + THIN)
        heads[rows] = packed([b[0] for b in both[t : t + PIECES]], 0)
        tails[rows] = packed([b[1] for b in both[t : t + PIECES]], HALF - DEPTH)


def folded(packed_masks):
    quarter = lax.shift_right_logical(lanes(), 5)
    out = packed_masks[:QUARTER]
    for b in range(1, 4):
        part = packed_masks[QUARTER * b : QUARTER * b + QUARTER]
        out = jnp.where(quarter == b, turn(part, COLS // 4 * (b % 2)), out)
    return out


def unfolded(quarters):
    low = lanes() < HALF
    parts = [jnp.where(low, turn(quarters, -32 * b), turn(quarters, HALF - 32 * b)) for b in range(4)]
    return jnp.concatenate(parts, axis=0)


def fetched(sources, targets, sems):
    copies = [pltpu.make_async_copy(s, t, sems.at[k]) for k, (s, t) in enumerate(zip(sources, targets))]
    for copy in copies:
        copy.start()
    for copy in copies:
        copy.wait()


def bond_masks(bonds, rows):
    last_x = lax.axis_index("gx") == lax.axis_size("gx") - 1
    last_y = lax.axis_index("gy") == lax.axis_size("gy") - 1
    down, side = (bonds[m, rows].astype(f32) for m in range(2))
    row = lax.broadcasted_iota(jnp.int32, down.shape, 0) + rows.start
    down = jnp.where(jnp.logical_and(last_x, row == ROWS - 1), 0.0, down)
    side = jnp.where(jnp.logical_and(last_y, lanes() == COLS - 1), 0.0, side)
    return down, side


def pack_rows(state_at, potential_at, bonds_at, to_prev, to_next, state, potential, bonds, sems):
    fetched((state_at, potential_at, bonds_at), (state, potential, bonds), sems)
    for ref, rows, skip in ((to_prev, slice(0, 16), 0), (to_next, slice(16, 32), 16 - DEPTH)):
        for f in range(FIELDS):
            part = state[f, rows].astype(f32)[skip : skip + DEPTH]
            ref[pl.ds(f, 8, stride=FIELDS), :] = part[:8]
            ref[8 * FIELDS + f : 8 * FIELDS + f + 1] = part[8:]
        down, side = bond_masks(bonds, rows)
        for m, value in enumerate((potential[rows], down, side)):
            ref[EDGE + 16 * m : EDGE + 16 * m + 16] = value


def turn_bulk(
    coeffs, boundary, phase, state_at, potential_at, bonds_at, wave, masks, heads, tails, own, consts,
    state, potential, bonds, sems,
):
    fetched((state_at, potential_at, bonds_at), (state, potential, bonds), sems)
    for f in range(FIELDS):
        wave[pl.ds(f, ROWS, stride=FIELDS), :] = state[f].astype(f32)
    down, side = bond_masks(bonds, slice(0, ROWS))
    for m, value in enumerate((potential[...], down, side)):
        masks[m] = value
    both = []
    for i in range(ROWS):
        both.append(ends_of(wave, FIELDS * i))
        own[THIN * i : THIN * i + THIN] = own_strip(*both[i])
    pack_places(both, 0, heads, tails)
    first_col = lax.axis_index("gy") * COLS
    consts[:3] = jnp.concatenate(factors(coeffs), axis=0)
    e3 = 4.0 * coeffs[3] / 125.0
    one = jnp.ones((1, COLS), f32)
    consts[3:4] = one * (e3 * e3 * e3)
    consts[4:5] = one * phase[0]
    consts[5:6] = one * phase[1]
    consts[6:7] = one * phase[2]
    consts[7:8] = (lanes() + first_col >= boundary[0]).astype(f32)


def tall_mask(masks, above, below, m):
    at = EDGE + 16 * m
    pad = jnp.zeros((TALL_PAD - TALL, COLS), f32)
    return jnp.concatenate([above[at + 16 - DEPTH : at + 16], masks[m], below[at : at + DEPTH], pad], axis=0)


def pack_columns(above, below, masks, heads, tails, off_chip, on_chip, own, own_masks, more_heads, more_tails):
    even = lax.axis_index("gy") % 2 == 0

    def send(rows, head, tail):
        on_chip[rows] = jnp.where(even, tail, head)
        off_chip[rows] = jnp.where(even, head, tail)

    both = [ends_of(ref, FIELDS * i) for ref in (above, below) for i in range(DEPTH)]
    for i in range(2 * DEPTH):
        own[THIN * i : THIN * i + THIN] = own_strip(*both[i])
    pack_places(both, 0, more_heads, more_tails)
    send(slice(0, THIN * OWN_PLACES), heads[...], tails[...])
    send(slice(THIN * OWN_PLACES, THIN * PLACES), more_heads[...], more_tails[...])
    parts = []
    for m in range(3):
        mask = tall_mask(masks, above, below, m)
        parts.append(ends(mask, mask))
        own_masks[m] = own_strip(*parts[m])
    off_chip[COL_MSG:] = jnp.zeros((MORE, COLS), f32)
    send(
        slice(THIN * PLACES, COL_MSG),
        folded(packed([p[0] for p in parts], 0)),
        folded(packed([p[1] for p in parts], HALF - DEPTH)),
    )


def spread_rows(spread, m, value, count=TALL):
    for i in range(count):
        spread[m, 8 * i : 8 * i + 8] = jnp.broadcast_to(value[i : i + 1], (8, COLS))


def hamilton(source, masks, wide, first, after, finish):
    many = BATCH if wide == THIN else 1

    def rows_of(i, some):
        return source[wide * i : wide * (i + some)].reshape(some, wide, COLS)

    def mask_of(m, i, some):
        one = masks[m, 8 * i : 8 * (i + some)].reshape(some, 8, COLS)
        return jnp.concatenate([one] * (wide // 8), axis=1)

    for i in range(first, after, many):
        some = min(many, after - i)
        here = rows_of(i, some)
        pot, down, side = (mask_of(m, i, some) for m in range(3))
        right = turn(here, -1)
        left = turn(side * here, 1)
        handed = mask_of(1, i - 1, some) * rows_of(i - 1, some)
        hop = (down * rows_of(i + 1, some) + handed) + (side * right + left)
        finish(slice(wide * i, wide * (i + some)), pot * here - hop)


def factors(coeffs):
    c0, c1, c2, c3 = (coeffs[k] for k in range(4))
    one = jnp.ones((1, COLS), f32)
    per = 1.0 / (one * (4.0 * c3 / 125.0))
    return one * (c0 + c2) * per, one * ((c1 + 3.0 * c3) / 5.0) * per, one * (2.0 * c2 / 25.0) * per


def step_of(start, out, one, two, masks, wide, d, weights):
    a0, a1, a2 = weights

    half = wide // 2

    def put(ref, rows, value):
        ref[rows] = value.reshape(-1, COLS)

    def get(ref, rows):
        return ref[rows].reshape(-1, wide, COLS)

    def first(rows, value):
        put(one, rows, value)

    def second(rows, value):
        x = get(start, rows)
        put(two, rows, a1 * x - value)
        put(out, rows, a0 * x - a2 * value)

    def third(rows, value):
        kept = get(out, rows)
        parts = [kept[:, :half] + value[:, half:], kept[:, half:] - value[:, :half]]
        put(out, rows, jnp.concatenate(parts, axis=1))

    hamilton(start, masks, wide, d + 1, TALL - d - 1, first)
    hamilton(one, masks, wide, d + 2, TALL - d - 2, second)
    hamilton(two, masks, wide, d + 3, TALL - d - 3, third)


def evolve_main(consts, wave, above, below, masks, main, spread, cur, one, two):
    for m in range(3):
        spread_rows(spread, m, tall_mask(masks, above, below, m))
    cur[:EDGE] = above[:EDGE]
    cur[EDGE : EDGE + ROWS * FIELDS] = wave[...]
    cur[EDGE + ROWS * FIELDS :] = below[:EDGE]
    weights = [consts[k : k + 1] for k in range(3)]
    for step in range(STEPS):
        step_of(cur, cur, one, two, spread, FIELDS, 3 * step, weights)
    main[...] = cur[EDGE : EDGE + ROWS * FIELDS]


def evolve_rest(
    consts, main, own, more_own, own_masks, on_chip, off_chip, evolved, part,
    strip, one, two, spread, cells, flat, fields, sem,
):
    even = lax.axis_index("gy") % 2 == 0

    def received(rows):
        a, b = on_chip[rows], off_chip[rows]
        return jnp.where(even, b, a), jnp.where(even, a, b)

    left, right = (unfolded(side) for side in received(slice(THIN * PLACES, COL_MSG)))
    for m in range(3):
        spread_rows(spread, m, join(left, own_masks[m], right, m))
    for t in range(PLACES):
        left, right = received(slice(THIN * t, THIN * t + THIN))
        for u in range(PIECES):
            i = PIECES * t + u
            ref = own if t < OWN_PLACES else more_own
            i = i if t < OWN_PLACES else i - PIECES * OWN_PLACES
            if THIN * i < ref.shape[0]:
                at = i + DEPTH if t < OWN_PLACES else (i if i < DEPTH else i + ROWS)
                value = join(left, ref[THIN * i : THIN * i + THIN], right, u)
                strip[THIN * at : THIN * at + THIN] = value

    weights = [consts[k : k + 1] for k in range(3)]
    for step in range(STEPS):
        step_of(strip, strip, one, two, spread, THIN, 3 * step, weights)

    scale = consts[3:4]
    for r in range(0, ROWS, CHUNK):
        rim = strip[THIN * (r + DEPTH) : THIN * (r + DEPTH + CHUNK)].reshape(CHUNK, THIN, COLS)
        rows = slice(FIELDS * r, FIELDS * (r + CHUNK))
        middle = main[rows].reshape(CHUNK, FIELDS, COLS)
        parts = []
        for g in range(GROUPS):
            mine, by = rim[:, 8 * (g // 2) : 8 * (g // 2) + 8], HALF * (g % 2)
            value = jnp.where(lanes() < DEPTH, turn(mine, -by - DEPTH), middle[:, 8 * g : 8 * g + 8])
            parts.append(jnp.where(lanes() >= COLS - DEPTH, turn(mine, HALF + DEPTH - by), value))
        done = jnp.concatenate(parts, axis=1) * scale
        cells[rows] = done.reshape(CHUNK * FIELDS, COLS)
    for f in range(FIELDS):
        fields[f] = cells[pl.ds(f, ROWS, stride=FIELDS), :].astype(jnp.bfloat16)
    leaving = pltpu.make_async_copy(fields, evolved, sem)
    leaving.start()
    for r in range(ROWS):
        flat[:, COLS * r : COLS * (r + 1)] = cells[FIELDS * r : FIELDS * (r + 1)].astype(jnp.bfloat16)

    inside = consts[7:8].astype(jnp.bfloat16)
    amps = flat[...]
    amps_right = jnp.concatenate([amps[:, COLS * r : COLS * r + COLS] * inside for r in range(ROWS)], axis=1)
    contract = (((1,), (1,)), ((), ()))
    total = lax.dot_general(amps, amps, contract, preferred_element_type=f32)
    right = lax.dot_general(amps, amps_right, contract, preferred_element_type=f32)
    n = FIELDS // 2
    total_re = total[:n, :n] + total[n:, n:]
    total_im = total[:n, n:] - total[n:, :n]
    right_re = right[:n, :n] + right[n:, n:]
    right_im = right[:n, n:] - right[n:, :n]
    cosine, sine, count = (consts[k : k + 1, :n] for k in (4, 5, 6))
    over_re = (total_re + cosine * right_re - sine * right_im) * count
    over_im = (total_im + cosine * right_im + sine * right_re) * count
    wide = jnp.concatenate([over_re, over_im], axis=0)
    tiles = [wide[8 * g : 8 * g + 8] for g in range(GROUPS)] + [jnp.zeros((8, COLS - GROUPS * n), f32)]
    tile = jnp.concatenate(tiles, axis=1)
    for p in range(part.shape[0]):
        part[p] = tile
    leaving.wait()


def call(kernel, outs, inputs, scalars=0, fetched=0, sent=0, scratch=(), limit=8, flops=100_000):
    many = len(inputs)
    shapes = [pltpu.VMEM(s, d) for s, d in scratch]
    shapes += [pltpu.VMEM(x.shape, x.dtype) for x in inputs[many - fetched :]]
    if fetched:
        shapes.append(pltpu.SemaphoreType.DMA((fetched,)))
    if sent:
        shapes.append(pltpu.SemaphoreType.DMA)
    spaces = [pltpu.SMEM] * scalars + [pltpu.VMEM] * (many - scalars - fetched) + [pltpu.HBM] * fetched
    return pl.pallas_call(
        kernel,
        out_shape=[jax.ShapeDtypeStruct(s, d) for s, d in outs],
        in_specs=[pl.BlockSpec(memory_space=space) for space in spaces],
        out_specs=[pl.BlockSpec(memory_space=pltpu.HBM if k < sent else pltpu.VMEM) for k in range(len(outs))],
        scratch_shapes=shapes,
        compiler_params=pltpu.CompilerParams(vmem_limit_bytes=limit * MIB),
        cost_estimate=pl.CostEstimate(flops=flops, bytes_accessed=sum(4 * x.size for x in inputs), transcendentals=0),
    )(*inputs)


def added(parts, axis):
    return jnp.sum(lax.all_to_all(parts, axis, 0, 0, tiled=True), axis=0)


def on_device(state, potential, bonds, coeffs, boundary, counting):
    norbit = state.shape[1]
    peers_x, peers_y = lax.axis_size("gx"), lax.axis_size("gy")
    count = float(ROWS * COLS * peers_x * peers_y)
    phase = jnp.stack([jnp.cos(counting[0]) - 1.0, jnp.sin(counting[0]), jnp.float32(1.0 / count)])
    fields = state.reshape(FIELDS, ROWS, COLS)

    inputs = (fields, potential, bonds)
    to_prev, to_next = call(pack_rows, [((ROW_MSG, COLS), f32)] * 2, inputs, fetched=3, limit=FIRST_LIMIT)
    above = lax.ppermute(to_next, "gx", [(i, (i + 1) % peers_x) for i in range(peers_x)])
    below = lax.ppermute(to_prev, "gx", [(i, (i - 1) % peers_x) for i in range(peers_x)])
    own_msg, more_msg = ((THIN * OWN_PLACES, COLS), f32), ((THIN * (PLACES - OWN_PLACES), COLS), f32)
    wave, masks, heads, tails, own, consts = call(
        turn_bulk,
        [
            ((ROWS * FIELDS, COLS), f32),
            ((3, ROWS, COLS), f32),
            own_msg,
            own_msg,
            ((THIN * ROWS, COLS), f32),
            ((8, COLS), f32),
        ],
        (coeffs, boundary, phase) + inputs,
        scalars=3,
        fetched=3,
    )
    tall, thin, spread = ((FIELDS * TALL, COLS), f32), ((THIN * TALL, COLS), f32), ((3, 8 * TALL, COLS), f32)
    off_chip, on_chip, more_own, own_masks = call(
        pack_columns,
        [
            ((COL_MSG + MORE, COLS), f32),
            ((COL_MSG, COLS), f32),
            ((THIN * 2 * DEPTH, COLS), f32),
            ((3, TALL_PAD, COLS), f32),
        ],
        (above, below, masks, heads, tails),
        scratch=[more_msg] * 2,
    )
    pairs = [(i, i + 2 * (i % 2) - 1) for i in range(1, peers_y - 1)]
    off_chip = lax.ppermute(off_chip, "gy", pairs)
    on_chip = lax.ppermute(on_chip, "gy", [(i, i ^ 1) for i in range(peers_y)])
    (main,) = call(
        evolve_main,
        [((FIELDS * ROWS, COLS), f32)],
        (consts, wave, above, below, masks),
        scratch=[spread] + [tall] * 3,
        limit=12,
        flops=20_000_000,
    )
    block = ((FIELDS, ROWS, COLS), jnp.bfloat16)
    evolved, part = call(
        evolve_rest,
        [block, ((peers_y, 8, COLS), f32)],
        (consts, main, own, more_own, own_masks, on_chip, off_chip),
        sent=1,
        scratch=[thin] * 3
        + [spread, ((FIELDS * ROWS, COLS), f32), ((FIELDS, ROWS * COLS), jnp.bfloat16), block],
        limit=12,
        flops=10_000_000,
    )
    total = added(part, "gy")
    total = added(jnp.broadcast_to(total[None], (peers_x,) + total.shape), "gx")
    over = total[:, : GROUPS * norbit].reshape(8, GROUPS, norbit).transpose(1, 0, 2).reshape(2, norbit, norbit)
    return evolved.reshape(state.shape), over


def solution(mesh):
    return jax.shard_map(
        on_device,
        mesh=mesh,
        in_specs=(P(None, None, "gx", "gy"), P("gx", "gy"), P(None, "gx", "gy"), P(), P(), P()),
        out_specs=(P(None, None, "gx", "gy"), P()),
        check_vma=False,
    )
```

```python
import jax
import jax.numpy as jnp
from jax import lax
from jax.experimental import pallas as pl
from jax.experimental.pallas import tpu as pltpu
from jax.sharding import PartitionSpec as P

STEPS = 3
DEPTH = 3 * STEPS
ROWS, COLS, FIELDS = 32, 128, 32
GROUPS = 4
HALF = COLS // 2
TALL = ROWS + 2 * DEPTH
TALL_PAD = 64
QUARTER = TALL_PAD // 4
BATCH = 16
CHUNK = 8
PIECES = 7
OWN_PLACES, PLACES = 5, 8
EDGE = DEPTH * FIELDS
THIN = 16
ROW_MSG = EDGE + 3 * 16
COL_MSG = THIN * PLACES + QUARTER
MORE = 8
PART = 4
MIB = 1024 * 1024
FIRST_LIMIT = 62

f32 = jnp.float32


def lanes():
    return lax.broadcasted_iota(jnp.int32, (1, COLS), 1)


def inner_lanes():
    return lanes() & (HALF - 1)


def turn(value, by):
    by = by % COLS
    return pltpu.roll(value, by, value.ndim - 1) if by else value


def ends(a, b):
    low = lanes() < HALF
    return jnp.where(low, a, turn(b, HALF)), jnp.where(low, turn(a, HALF), b)


def own_strip(head, tail):
    return jnp.where(inner_lanes() < HALF // 2, turn(head, DEPTH), turn(tail, -DEPTH))


def packed(parts, first):
    out = turn(parts[0], -first)
    for u in range(1, len(parts)):
        out = jnp.where(inner_lanes() < DEPTH * u, out, turn(parts[u], DEPTH * u - first))
    return out


def join(from_left, own, from_right, u):
    inner = inner_lanes()
    left = turn(from_left, -DEPTH * u)
    right = turn(from_right, HALF - DEPTH - DEPTH * u)
    return jnp.where(inner < DEPTH, left, jnp.where(inner < HALF - DEPTH, own, right))


def ends_of(ref, at):
    groups = [ref[at + 8 * g : at + 8 * g + 8] for g in range(GROUPS)]
    both = [ends(groups[2 * p], groups[2 * p + 1]) for p in range(2)]
    return tuple(jnp.concatenate([pair[k] for pair in both], axis=0) for k in range(2))


def pack_places(both, first, heads, tails):
    for t in range(0, len(both), PIECES):
        rows = slice(THIN * (first + t // PIECES), THIN * (first + t // PIECES) + THIN)
        heads[rows] = packed([b[0] for b in both[t : t + PIECES]], 0)
        tails[rows] = packed([b[1] for b in both[t : t + PIECES]], HALF - DEPTH)


def folded(packed_masks):
    quarter = lax.shift_right_logical(lanes(), 5)
    out = packed_masks[:QUARTER]
    for b in range(1, 4):
        part = packed_masks[QUARTER * b : QUARTER * b + QUARTER]
        out = jnp.where(quarter == b, turn(part, COLS // 4 * (b % 2)), out)
    return out


def unfolded(quarters):
    low = lanes() < HALF
    parts = [jnp.where(low, turn(quarters, -32 * b), turn(quarters, HALF - 32 * b)) for b in range(4)]
    return jnp.concatenate(parts, axis=0)


def fetched(sources, targets, sems):
    copies = [pltpu.make_async_copy(s, t, sems.at[k]) for k, (s, t) in enumerate(zip(sources, targets))]
    for copy in copies:
        copy.start()
    for copy in copies:
        copy.wait()


def bond_masks(bonds, rows):
    last_x = lax.axis_index("gx") == lax.axis_size("gx") - 1
    last_y = lax.axis_index("gy") == lax.axis_size("gy") - 1
    down, side = (bonds[m, rows].astype(f32) for m in range(2))
    row = lax.broadcasted_iota(jnp.int32, down.shape, 0) + rows.start
    down = jnp.where(jnp.logical_and(last_x, row == ROWS - 1), 0.0, down)
    side = jnp.where(jnp.logical_and(last_y, lanes() == COLS - 1), 0.0, side)
    return down, side


def pack_rows(state_at, potential_at, bonds_at, to_prev, to_next, state, potential, bonds, sems):
    fetched((state_at, potential_at, bonds_at), (state, potential, bonds), sems)
    for ref, rows, skip in ((to_prev, slice(0, 16), 0), (to_next, slice(16, 32), 16 - DEPTH)):
        for f in range(FIELDS):
            part = state[f, rows].astype(f32)[skip : skip + DEPTH]
            ref[pl.ds(f, 8, stride=FIELDS), :] = part[:8]
            ref[8 * FIELDS + f : 8 * FIELDS + f + 1] = part[8:]
        down, side = bond_masks(bonds, rows)
        for m, value in enumerate((potential[rows], down, side)):
            ref[EDGE + 16 * m : EDGE + 16 * m + 16] = value


def turn_bulk(
    coeffs, boundary, phase, state_at, potential_at, bonds_at, wave, masks, heads, tails, own, consts,
    state, potential, bonds, sems,
):
    fetched((state_at, potential_at, bonds_at), (state, potential, bonds), sems)
    for f in range(FIELDS):
        wave[pl.ds(f, ROWS, stride=FIELDS), :] = state[f].astype(f32)
    down, side = bond_masks(bonds, slice(0, ROWS))
    for m, value in enumerate((potential[...], down, side)):
        masks[m] = value
    both = []
    for i in range(ROWS):
        both.append(ends_of(wave, FIELDS * i))
        own[THIN * i : THIN * i + THIN] = own_strip(*both[i])
    pack_places(both, 0, heads, tails)
    first_col = lax.axis_index("gy") * COLS
    consts[:3] = jnp.concatenate(factors(coeffs), axis=0)
    e3 = 4.0 * coeffs[3] / 125.0
    one = jnp.ones((1, COLS), f32)
    consts[3:4] = one * (e3 * e3 * e3)
    consts[4:5] = one * phase[0]
    consts[5:6] = one * phase[1]
    consts[6:7] = one * phase[2]
    consts[7:8] = (lanes() + first_col >= boundary[0]).astype(f32)


def tall_mask(masks, above, below, m):
    at = EDGE + 16 * m
    pad = jnp.zeros((TALL_PAD - TALL, COLS), f32)
    return jnp.concatenate([above[at + 16 - DEPTH : at + 16], masks[m], below[at : at + DEPTH], pad], axis=0)


def pack_columns(above, below, masks, heads, tails, off_chip, on_chip, own, own_masks, more_heads, more_tails):
    even = lax.axis_index("gy") % 2 == 0

    def send(rows, head, tail):
        on_chip[rows] = jnp.where(even, tail, head)
        off_chip[rows] = jnp.where(even, head, tail)

    both = [ends_of(ref, FIELDS * i) for ref in (above, below) for i in range(DEPTH)]
    for i in range(2 * DEPTH):
        own[THIN * i : THIN * i + THIN] = own_strip(*both[i])
    pack_places(both, 0, more_heads, more_tails)
    send(slice(0, THIN * OWN_PLACES), heads[...], tails[...])
    send(slice(THIN * OWN_PLACES, THIN * PLACES), more_heads[...], more_tails[...])
    parts = []
    for m in range(3):
        mask = tall_mask(masks, above, below, m)
        parts.append(ends(mask, mask))
        own_masks[m] = own_strip(*parts[m])
    off_chip[COL_MSG:] = jnp.zeros((MORE, COLS), f32)
    send(
        slice(THIN * PLACES, COL_MSG),
        folded(packed([p[0] for p in parts], 0)),
        folded(packed([p[1] for p in parts], HALF - DEPTH)),
    )


def spread_rows(spread, m, value, count=TALL):
    for i in range(count):
        spread[m, 8 * i : 8 * i + 8] = jnp.broadcast_to(value[i : i + 1], (8, COLS))


def hamilton(source, masks, wide, first, after, finish):
    many = BATCH if wide == THIN else 1

    def rows_of(i, some):
        return source[wide * i : wide * (i + some)].reshape(some, wide, COLS)

    def mask_of(m, i, some):
        one = masks[m, 8 * i : 8 * (i + some)].reshape(some, 8, COLS)
        return jnp.concatenate([one] * (wide // 8), axis=1)

    for i in range(first, after, many):
        some = min(many, after - i)
        here = rows_of(i, some)
        pot, down, side = (mask_of(m, i, some) for m in range(3))
        right = turn(here, -1)
        left = turn(side * here, 1)
        handed = mask_of(1, i - 1, some) * rows_of(i - 1, some)
        hop = (down * rows_of(i + 1, some) + handed) + (side * right + left)
        finish(slice(wide * i, wide * (i + some)), pot * here - hop)


def factors(coeffs):
    c0, c1, c2, c3 = (coeffs[k] for k in range(4))
    one = jnp.ones((1, COLS), f32)
    per = 1.0 / (one * (4.0 * c3 / 125.0))
    return one * (c0 + c2) * per, one * ((c1 + 3.0 * c3) / 5.0) * per, one * (2.0 * c2 / 25.0) * per


def step_of(start, out, one, two, masks, wide, d, weights):
    a0, a1, a2 = weights

    half = wide // 2

    def put(ref, rows, value):
        ref[rows] = value.reshape(-1, COLS)

    def get(ref, rows):
        return ref[rows].reshape(-1, wide, COLS)

    def first(rows, value):
        put(one, rows, value)

    def second(rows, value):
        x = get(start, rows)
        put(two, rows, a1 * x - value)
        put(out, rows, a0 * x - a2 * value)

    def third(rows, value):
        kept = get(out, rows)
        parts = [kept[:, :half] + value[:, half:], kept[:, half:] - value[:, :half]]
        put(out, rows, jnp.concatenate(parts, axis=1))

    hamilton(start, masks, wide, d + 1, TALL - d - 1, first)
    hamilton(one, masks, wide, d + 2, TALL - d - 2, second)
    hamilton(two, masks, wide, d + 3, TALL - d - 3, third)


def evolve_main(consts, wave, above, below, masks, main, spread, cur, one, two):
    for m in range(3):
        spread_rows(spread, m, tall_mask(masks, above, below, m))
    cur[:EDGE] = above[:EDGE]
    cur[EDGE : EDGE + ROWS * FIELDS] = wave[...]
    cur[EDGE + ROWS * FIELDS :] = below[:EDGE]
    weights = [consts[k : k + 1] for k in range(3)]
    for step in range(STEPS):
        step_of(cur, cur, one, two, spread, FIELDS, 3 * step, weights)
    main[...] = cur[EDGE : EDGE + ROWS * FIELDS]


def evolve_rest(
    consts, main, own, more_own, own_masks, on_chip, off_chip, evolved, part,
    strip, one, two, spread, cells, flat, fields, sem,
):
    even = lax.axis_index("gy") % 2 == 0

    def received(rows):
        a, b = on_chip[rows], off_chip[rows]
        return jnp.where(even, b, a), jnp.where(even, a, b)

    left, right = (unfolded(side) for side in received(slice(THIN * PLACES, COL_MSG)))
    for m in range(3):
        spread_rows(spread, m, join(left, own_masks[m], right, m))
    for t in range(PLACES):
        left, right = received(slice(THIN * t, THIN * t + THIN))
        for u in range(PIECES):
            i = PIECES * t + u
            ref = own if t < OWN_PLACES else more_own
            i = i if t < OWN_PLACES else i - PIECES * OWN_PLACES
            if THIN * i < ref.shape[0]:
                at = i + DEPTH if t < OWN_PLACES else (i if i < DEPTH else i + ROWS)
                value = join(left, ref[THIN * i : THIN * i + THIN], right, u)
                strip[THIN * at : THIN * at + THIN] = value

    weights = [consts[k : k + 1] for k in range(3)]
    for step in range(STEPS):
        step_of(strip, strip, one, two, spread, THIN, 3 * step, weights)

    scale = consts[3:4]
    for r in range(0, ROWS, CHUNK):
        rim = strip[THIN * (r + DEPTH) : THIN * (r + DEPTH + CHUNK)].reshape(CHUNK, THIN, COLS)
        rows = slice(FIELDS * r, FIELDS * (r + CHUNK))
        middle = main[rows].reshape(CHUNK, FIELDS, COLS)
        parts = []
        for g in range(GROUPS):
            mine, by = rim[:, 8 * (g // 2) : 8 * (g // 2) + 8], HALF * (g % 2)
            value = jnp.where(lanes() < DEPTH, turn(mine, -by - DEPTH), middle[:, 8 * g : 8 * g + 8])
            parts.append(jnp.where(lanes() >= COLS - DEPTH, turn(mine, HALF + DEPTH - by), value))
        done = jnp.concatenate(parts, axis=1) * scale
        cells[rows] = done.reshape(CHUNK * FIELDS, COLS)
    for f in range(FIELDS):
        fields[f] = cells[pl.ds(f, ROWS, stride=FIELDS), :].astype(jnp.bfloat16)
    leaving = pltpu.make_async_copy(fields, evolved, sem)
    leaving.start()
    for r in range(ROWS):
        flat[:, COLS * r : COLS * (r + 1)] = cells[FIELDS * r : FIELDS * (r + 1)].astype(jnp.bfloat16)

    inside = consts[7:8].astype(jnp.bfloat16)
    amps = flat[...]
    amps_right = jnp.concatenate([amps[:, COLS * r : COLS * r + COLS] * inside for r in range(ROWS)], axis=1)
    contract = (((1,), (1,)), ((), ()))
    total = lax.dot_general(amps, amps, contract, preferred_element_type=f32)
    right = lax.dot_general(amps, amps_right, contract, preferred_element_type=f32)
    n = FIELDS // 2
    total_re = total[:n, :n] + total[n:, n:]
    total_im = total[:n, n:] - total[n:, :n]
    right_re = right[:n, :n] + right[n:, n:]
    right_im = right[:n, n:] - right[n:, :n]
    cosine, sine, count = (consts[k : k + 1, :n] for k in (4, 5, 6))
    over_re = (total_re + cosine * right_re - sine * right_im) * count
    over_im = (total_im + cosine * right_im + sine * right_re) * count
    wide = jnp.concatenate([over_re, over_im], axis=0)
    rows = [wide[8 * g : 8 * g + 8] for g in range(GROUPS)]
    eight = jnp.concatenate(rows + rows, axis=1)
    tile = jnp.where(lanes() < HALF, eight[:PART], eight[PART:])
    for p in range(part.shape[0]):
        part[p] = tile
    leaving.wait()


def call(kernel, outs, inputs, scalars=0, fetched=0, sent=0, scratch=(), limit=8, flops=100_000):
    many = len(inputs)
    shapes = [pltpu.VMEM(s, d) for s, d in scratch]
    shapes += [pltpu.VMEM(x.shape, x.dtype) for x in inputs[many - fetched :]]
    if fetched:
        shapes.append(pltpu.SemaphoreType.DMA((fetched,)))
    if sent:
        shapes.append(pltpu.SemaphoreType.DMA)
    spaces = [pltpu.SMEM] * scalars + [pltpu.VMEM] * (many - scalars - fetched) + [pltpu.HBM] * fetched
    return pl.pallas_call(
        kernel,
        out_shape=[jax.ShapeDtypeStruct(s, d) for s, d in outs],
        in_specs=[pl.BlockSpec(memory_space=space) for space in spaces],
        out_specs=[pl.BlockSpec(memory_space=pltpu.HBM if k < sent else pltpu.VMEM) for k in range(len(outs))],
        scratch_shapes=shapes,
        compiler_params=pltpu.CompilerParams(vmem_limit_bytes=limit * MIB),
        cost_estimate=pl.CostEstimate(flops=flops, bytes_accessed=sum(4 * x.size for x in inputs), transcendentals=0),
    )(*inputs)


def added(parts, axis):
    return jnp.sum(lax.all_to_all(parts, axis, 0, 0, tiled=True), axis=0)


def on_device(state, potential, bonds, coeffs, boundary, counting):
    norbit = state.shape[1]
    peers_x, peers_y = lax.axis_size("gx"), lax.axis_size("gy")
    count = float(ROWS * COLS * peers_x * peers_y)
    phase = jnp.stack([jnp.cos(counting[0]) - 1.0, jnp.sin(counting[0]), jnp.float32(1.0 / count)])
    fields = state.reshape(FIELDS, ROWS, COLS)

    inputs = (fields, potential, bonds)
    to_prev, to_next = call(pack_rows, [((ROW_MSG, COLS), f32)] * 2, inputs, fetched=3, limit=FIRST_LIMIT)
    above = lax.ppermute(to_next, "gx", [(i, (i + 1) % peers_x) for i in range(peers_x)])
    below = lax.ppermute(to_prev, "gx", [(i, (i - 1) % peers_x) for i in range(peers_x)])
    own_msg, more_msg = ((THIN * OWN_PLACES, COLS), f32), ((THIN * (PLACES - OWN_PLACES), COLS), f32)
    wave, masks, heads, tails, own, consts = call(
        turn_bulk,
        [
            ((ROWS * FIELDS, COLS), f32),
            ((3, ROWS, COLS), f32),
            own_msg,
            own_msg,
            ((THIN * ROWS, COLS), f32),
            ((8, COLS), f32),
        ],
        (coeffs, boundary, phase) + inputs,
        scalars=3,
        fetched=3,
    )
    tall, thin, spread = ((FIELDS * TALL, COLS), f32), ((THIN * TALL, COLS), f32), ((3, 8 * TALL, COLS), f32)
    off_chip, on_chip, more_own, own_masks = call(
        pack_columns,
        [
            ((COL_MSG + MORE, COLS), f32),
            ((COL_MSG, COLS), f32),
            ((THIN * 2 * DEPTH, COLS), f32),
            ((3, TALL_PAD, COLS), f32),
        ],
        (above, below, masks, heads, tails),
        scratch=[more_msg] * 2,
    )
    pairs = [(i, i + 2 * (i % 2) - 1) for i in range(1, peers_y - 1)]
    off_chip = lax.ppermute(off_chip, "gy", pairs)
    on_chip = lax.ppermute(on_chip, "gy", [(i, i ^ 1) for i in range(peers_y)])
    (main,) = call(
        evolve_main,
        [((FIELDS * ROWS, COLS), f32)],
        (consts, wave, above, below, masks),
        scratch=[spread] + [tall] * 3,
        limit=12,
        flops=20_000_000,
    )
    block = ((FIELDS, ROWS, COLS), jnp.bfloat16)
    evolved, part = call(
        evolve_rest,
        [block, ((peers_y, PART, COLS), f32)],
        (consts, main, own, more_own, own_masks, on_chip, off_chip),
        sent=1,
        scratch=[thin] * 3
        + [spread, ((FIELDS * ROWS, COLS), f32), ((FIELDS, ROWS * COLS), jnp.bfloat16), block],
        limit=12,
        flops=10_000_000,
    )
    total = added(part, "gy")
    total = added(jnp.broadcast_to(total[None], (peers_x,) + total.shape), "gx")
    over = total.reshape(PART, 2, GROUPS, norbit).transpose(2, 1, 0, 3).reshape(2, norbit, norbit)
    return evolved.reshape(state.shape), over


def solution(mesh):
    return jax.shard_map(
        on_device,
        mesh=mesh,
        in_specs=(P(None, None, "gx", "gy"), P("gx", "gy"), P(None, "gx", "gy"), P(), P(), P()),
        out_specs=(P(None, None, "gx", "gy"), P()),
        check_vma=False,
    )
```

```python
import jax
import jax.numpy as jnp
from jax import lax
from jax.experimental import pallas as pl
from jax.experimental.pallas import tpu as pltpu
from jax.sharding import PartitionSpec as P

STEPS = 3
DEPTH = 3 * STEPS
ROWS, COLS, FIELDS = 32, 128, 32
GROUPS = 4
HALF = COLS // 2
TALL = ROWS + 2 * DEPTH
TALL_PAD = 64
QUARTER = TALL_PAD // 4
BATCH = 16
CHUNK = 8
PIECES = 7
OWN_PLACES, PLACES = 5, 8
EDGE = DEPTH * FIELDS
THIN = 16
ROW_MSG = EDGE + 32
COL_MSG = THIN * PLACES + QUARTER
MORE = 8
PART = 4
MIB = 1024 * 1024
FIRST_LIMIT = 62

f32 = jnp.float32


def lanes():
    return lax.broadcasted_iota(jnp.int32, (1, COLS), 1)


def inner_lanes():
    return lanes() & (HALF - 1)


def turn(value, by):
    by = by % COLS
    return pltpu.roll(value, by, value.ndim - 1) if by else value


def ends(a, b):
    low = lanes() < HALF
    return jnp.where(low, a, turn(b, HALF)), jnp.where(low, turn(a, HALF), b)


def own_strip(head, tail):
    return jnp.where(inner_lanes() < HALF // 2, turn(head, DEPTH), turn(tail, -DEPTH))


def packed(parts, first):
    out = turn(parts[0], -first)
    for u in range(1, len(parts)):
        out = jnp.where(inner_lanes() < DEPTH * u, out, turn(parts[u], DEPTH * u - first))
    return out


def join(from_left, own, from_right, u):
    inner = inner_lanes()
    left = turn(from_left, -DEPTH * u)
    right = turn(from_right, HALF - DEPTH - DEPTH * u)
    return jnp.where(inner < DEPTH, left, jnp.where(inner < HALF - DEPTH, own, right))


def ends_of(ref, at):
    groups = [ref[at + 8 * g : at + 8 * g + 8] for g in range(GROUPS)]
    both = [ends(groups[2 * p], groups[2 * p + 1]) for p in range(2)]
    return tuple(jnp.concatenate([pair[k] for pair in both], axis=0) for k in range(2))


def pack_places(both, first, heads, tails):
    for t in range(0, len(both), PIECES):
        rows = slice(THIN * (first + t // PIECES), THIN * (first + t // PIECES) + THIN)
        heads[rows] = packed([b[0] for b in both[t : t + PIECES]], 0)
        tails[rows] = packed([b[1] for b in both[t : t + PIECES]], HALF - DEPTH)


def folded(packed_masks):
    quarter = lax.shift_right_logical(lanes(), 5)
    out = packed_masks[:QUARTER]
    for b in range(1, 4):
        part = packed_masks[QUARTER * b : QUARTER * b + QUARTER]
        out = jnp.where(quarter == b, turn(part, COLS // 4 * (b % 2)), out)
    return out


def unfolded(quarters):
    low = lanes() < HALF
    parts = [jnp.where(low, turn(quarters, -32 * b), turn(quarters, HALF - 32 * b)) for b in range(4)]
    return jnp.concatenate(parts, axis=0)


def fetched(sources, targets, sems):
    copies = [pltpu.make_async_copy(s, t, sems.at[k]) for k, (s, t) in enumerate(zip(sources, targets))]
    for copy in copies:
        copy.start()
    for copy in copies:
        copy.wait()


def bond_masks(bonds, rows):
    last_x = lax.axis_index("gx") == lax.axis_size("gx") - 1
    last_y = lax.axis_index("gy") == lax.axis_size("gy") - 1
    down, side = (bonds[m, rows].astype(f32) for m in range(2))
    row = lax.broadcasted_iota(jnp.int32, down.shape, 0) + rows.start
    down = jnp.where(jnp.logical_and(last_x, row == ROWS - 1), 0.0, down)
    side = jnp.where(jnp.logical_and(last_y, lanes() == COLS - 1), 0.0, side)
    return down, side


def pack_rows(state_at, potential_at, bonds_at, to_prev, to_next, state, potential, bonds, sems):
    fetched((state_at, potential_at, bonds_at), (state, potential, bonds), sems)
    for ref, rows, skip in ((to_prev, slice(0, 16), 0), (to_next, slice(16, 32), 16 - DEPTH)):
        for f in range(FIELDS):
            part = state[f, rows].astype(f32)[skip : skip + DEPTH]
            ref[pl.ds(f, 8, stride=FIELDS), :] = part[:8]
            ref[8 * FIELDS + f : 8 * FIELDS + f + 1] = part[8:]
        down, side = bond_masks(bonds, rows)
        for m, value in enumerate((potential[rows], down, side)):
            ref[EDGE + DEPTH * m : EDGE + DEPTH * m + DEPTH] = value[skip : skip + DEPTH]
        ref[EDGE + 3 * DEPTH :] = jnp.zeros((ROW_MSG - EDGE - 3 * DEPTH, COLS), f32)


def turn_bulk(
    coeffs, boundary, phase, state_at, potential_at, bonds_at, wave, masks, heads, tails, own, consts,
    state, potential, bonds, sems,
):
    fetched((state_at, potential_at, bonds_at), (state, potential, bonds), sems)
    for f in range(FIELDS):
        wave[pl.ds(f, ROWS, stride=FIELDS), :] = state[f].astype(f32)
    down, side = bond_masks(bonds, slice(0, ROWS))
    for m, value in enumerate((potential[...], down, side)):
        masks[m] = value
    both = []
    for i in range(ROWS):
        both.append(ends_of(wave, FIELDS * i))
        own[THIN * i : THIN * i + THIN] = own_strip(*both[i])
    pack_places(both, 0, heads, tails)
    first_col = lax.axis_index("gy") * COLS
    consts[:3] = jnp.concatenate(factors(coeffs), axis=0)
    e3 = 4.0 * coeffs[3] / 125.0
    one = jnp.ones((1, COLS), f32)
    consts[3:4] = one * (e3 * e3 * e3)
    consts[4:5] = one * phase[0]
    consts[5:6] = one * phase[1]
    consts[6:7] = one * phase[2]
    consts[7:8] = (lanes() + first_col >= boundary[0]).astype(f32)


def tall_mask(masks, above, below, m):
    at = EDGE + DEPTH * m
    pad = jnp.zeros((TALL_PAD - TALL, COLS), f32)
    return jnp.concatenate([above[at : at + DEPTH], masks[m], below[at : at + DEPTH], pad], axis=0)


def pack_columns(above, below, masks, heads, tails, off_chip, on_chip, own, own_masks, more_heads, more_tails):
    even = lax.axis_index("gy") % 2 == 0

    def send(rows, head, tail):
        on_chip[rows] = jnp.where(even, tail, head)
        off_chip[rows] = jnp.where(even, head, tail)

    both = [ends_of(ref, FIELDS * i) for ref in (above, below) for i in range(DEPTH)]
    for i in range(2 * DEPTH):
        own[THIN * i : THIN * i + THIN] = own_strip(*both[i])
    pack_places(both, 0, more_heads, more_tails)
    send(slice(0, THIN * OWN_PLACES), heads[...], tails[...])
    send(slice(THIN * OWN_PLACES, THIN * PLACES), more_heads[...], more_tails[...])
    parts = []
    for m in range(3):
        mask = tall_mask(masks, above, below, m)
        parts.append(ends(mask, mask))
        own_masks[m] = own_strip(*parts[m])
    off_chip[COL_MSG:] = jnp.zeros((MORE, COLS), f32)
    send(
        slice(THIN * PLACES, COL_MSG),
        folded(packed([p[0] for p in parts], 0)),
        folded(packed([p[1] for p in parts], HALF - DEPTH)),
    )


def spread_rows(spread, m, value, count=TALL):
    for i in range(count):
        spread[m, 8 * i : 8 * i + 8] = jnp.broadcast_to(value[i : i + 1], (8, COLS))


def hamilton(source, masks, wide, first, after, finish):
    many = BATCH if wide == THIN else 1

    def rows_of(i, some):
        return source[wide * i : wide * (i + some)].reshape(some, wide, COLS)

    def mask_of(m, i, some):
        one = masks[m, 8 * i : 8 * (i + some)].reshape(some, 8, COLS)
        return jnp.concatenate([one] * (wide // 8), axis=1)

    for i in range(first, after, many):
        some = min(many, after - i)
        here = rows_of(i, some)
        pot, down, side = (mask_of(m, i, some) for m in range(3))
        right = turn(here, -1)
        left = turn(side * here, 1)
        handed = mask_of(1, i - 1, some) * rows_of(i - 1, some)
        hop = (down * rows_of(i + 1, some) + handed) + (side * right + left)
        finish(slice(wide * i, wide * (i + some)), pot * here - hop)


def factors(coeffs):
    c0, c1, c2, c3 = (coeffs[k] for k in range(4))
    one = jnp.ones((1, COLS), f32)
    per = 1.0 / (one * (4.0 * c3 / 125.0))
    return one * (c0 + c2) * per, one * ((c1 + 3.0 * c3) / 5.0) * per, one * (2.0 * c2 / 25.0) * per


def step_of(start, out, one, two, masks, wide, d, weights):
    a0, a1, a2 = weights

    half = wide // 2

    def put(ref, rows, value):
        ref[rows] = value.reshape(-1, COLS)

    def get(ref, rows):
        return ref[rows].reshape(-1, wide, COLS)

    def first(rows, value):
        put(one, rows, value)

    def second(rows, value):
        x = get(start, rows)
        put(two, rows, a1 * x - value)
        put(out, rows, a0 * x - a2 * value)

    def third(rows, value):
        kept = get(out, rows)
        parts = [kept[:, :half] + value[:, half:], kept[:, half:] - value[:, :half]]
        put(out, rows, jnp.concatenate(parts, axis=1))

    hamilton(start, masks, wide, d + 1, TALL - d - 1, first)
    hamilton(one, masks, wide, d + 2, TALL - d - 2, second)
    hamilton(two, masks, wide, d + 3, TALL - d - 3, third)


def evolve_main(consts, wave, above, below, masks, main, spread, cur, one, two):
    for m in range(3):
        spread_rows(spread, m, tall_mask(masks, above, below, m))
    cur[:EDGE] = above[:EDGE]
    cur[EDGE : EDGE + ROWS * FIELDS] = wave[...]
    cur[EDGE + ROWS * FIELDS :] = below[:EDGE]
    weights = [consts[k : k + 1] for k in range(3)]
    for step in range(STEPS):
        step_of(cur, cur, one, two, spread, FIELDS, 3 * step, weights)
    main[...] = cur[EDGE : EDGE + ROWS * FIELDS]


def evolve_rest(
    consts, main, own, more_own, own_masks, on_chip, off_chip, evolved, part,
    strip, one, two, spread, cells, flat, fields, sem,
):
    even = lax.axis_index("gy") % 2 == 0

    def received(rows):
        a, b = on_chip[rows], off_chip[rows]
        return jnp.where(even, b, a), jnp.where(even, a, b)

    left, right = (unfolded(side) for side in received(slice(THIN * PLACES, COL_MSG)))
    for m in range(3):
        spread_rows(spread, m, join(left, own_masks[m], right, m))
    for t in range(PLACES):
        left, right = received(slice(THIN * t, THIN * t + THIN))
        for u in range(PIECES):
            i = PIECES * t + u
            ref = own if t < OWN_PLACES else more_own
            i = i if t < OWN_PLACES else i - PIECES * OWN_PLACES
            if THIN * i < ref.shape[0]:
                at = i + DEPTH if t < OWN_PLACES else (i if i < DEPTH else i + ROWS)
                value = join(left, ref[THIN * i : THIN * i + THIN], right, u)
                strip[THIN * at : THIN * at + THIN] = value

    weights = [consts[k : k + 1] for k in range(3)]
    for step in range(STEPS):
        step_of(strip, strip, one, two, spread, THIN, 3 * step, weights)

    scale = consts[3:4]
    for r in range(0, ROWS, CHUNK):
        rim = strip[THIN * (r + DEPTH) : THIN * (r + DEPTH + CHUNK)].reshape(CHUNK, THIN, COLS)
        rows = slice(FIELDS * r, FIELDS * (r + CHUNK))
        middle = main[rows].reshape(CHUNK, FIELDS, COLS)
        parts = []
        for g in range(GROUPS):
            mine, by = rim[:, 8 * (g // 2) : 8 * (g // 2) + 8], HALF * (g % 2)
            value = jnp.where(lanes() < DEPTH, turn(mine, -by - DEPTH), middle[:, 8 * g : 8 * g + 8])
            parts.append(jnp.where(lanes() >= COLS - DEPTH, turn(mine, HALF + DEPTH - by), value))
        done = jnp.concatenate(parts, axis=1) * scale
        cells[rows] = done.reshape(CHUNK * FIELDS, COLS)
    for f in range(FIELDS):
        fields[f] = cells[pl.ds(f, ROWS, stride=FIELDS), :].astype(jnp.bfloat16)
    leaving = pltpu.make_async_copy(fields, evolved, sem)
    leaving.start()
    for r in range(ROWS):
        flat[:, COLS * r : COLS * (r + 1)] = cells[FIELDS * r : FIELDS * (r + 1)].astype(jnp.bfloat16)

    inside = consts[7:8].astype(jnp.bfloat16)
    amps = flat[...]
    amps_right = jnp.concatenate([amps[:, COLS * r : COLS * r + COLS] * inside for r in range(ROWS)], axis=1)
    contract = (((1,), (1,)), ((), ()))
    total = lax.dot_general(amps, amps, contract, preferred_element_type=f32)
    right = lax.dot_general(amps, amps_right, contract, preferred_element_type=f32)
    n = FIELDS // 2
    total_re = total[:n, :n] + total[n:, n:]
    total_im = total[:n, n:] - total[n:, :n]
    right_re = right[:n, :n] + right[n:, n:]
    right_im = right[:n, n:] - right[n:, :n]
    cosine, sine, count = (consts[k : k + 1, :n] for k in (4, 5, 6))
    over_re = (total_re + cosine * right_re - sine * right_im) * count
    over_im = (total_im + cosine * right_im + sine * right_re) * count
    wide = jnp.concatenate([over_re, over_im], axis=0)
    rows = [wide[8 * g : 8 * g + 8] for g in range(GROUPS)]
    eight = jnp.concatenate(rows + rows, axis=1)
    tile = jnp.where(lanes() < HALF, eight[:PART], eight[PART:])
    for p in range(part.shape[0]):
        part[p] = tile
    leaving.wait()


def call(kernel, outs, inputs, scalars=0, fetched=0, sent=0, scratch=(), limit=8, flops=100_000):
    many = len(inputs)
    shapes = [pltpu.VMEM(s, d) for s, d in scratch]
    shapes += [pltpu.VMEM(x.shape, x.dtype) for x in inputs[many - fetched :]]
    if fetched:
        shapes.append(pltpu.SemaphoreType.DMA((fetched,)))
    if sent:
        shapes.append(pltpu.SemaphoreType.DMA)
    spaces = [pltpu.SMEM] * scalars + [pltpu.VMEM] * (many - scalars - fetched) + [pltpu.HBM] * fetched
    return pl.pallas_call(
        kernel,
        out_shape=[jax.ShapeDtypeStruct(s, d) for s, d in outs],
        in_specs=[pl.BlockSpec(memory_space=space) for space in spaces],
        out_specs=[pl.BlockSpec(memory_space=pltpu.HBM if k < sent else pltpu.VMEM) for k in range(len(outs))],
        scratch_shapes=shapes,
        compiler_params=pltpu.CompilerParams(vmem_limit_bytes=limit * MIB),
        cost_estimate=pl.CostEstimate(flops=flops, bytes_accessed=sum(4 * x.size for x in inputs), transcendentals=0),
    )(*inputs)


def added(parts, axis):
    return jnp.sum(lax.all_to_all(parts, axis, 0, 0, tiled=True), axis=0)


def on_device(state, potential, bonds, coeffs, boundary, counting):
    norbit = state.shape[1]
    peers_x, peers_y = lax.axis_size("gx"), lax.axis_size("gy")
    count = float(ROWS * COLS * peers_x * peers_y)
    phase = jnp.stack([jnp.cos(counting[0]) - 1.0, jnp.sin(counting[0]), jnp.float32(1.0 / count)])
    fields = state.reshape(FIELDS, ROWS, COLS)

    inputs = (fields, potential, bonds)
    to_prev, to_next = call(pack_rows, [((ROW_MSG, COLS), f32)] * 2, inputs, fetched=3, limit=FIRST_LIMIT)
    above = lax.ppermute(to_next, "gx", [(i, (i + 1) % peers_x) for i in range(peers_x)])
    below = lax.ppermute(to_prev, "gx", [(i, (i - 1) % peers_x) for i in range(peers_x)])
    own_msg, more_msg = ((THIN * OWN_PLACES, COLS), f32), ((THIN * (PLACES - OWN_PLACES), COLS), f32)
    wave, masks, heads, tails, own, consts = call(
        turn_bulk,
        [
            ((ROWS * FIELDS, COLS), f32),
            ((3, ROWS, COLS), f32),
            own_msg,
            own_msg,
            ((THIN * ROWS, COLS), f32),
            ((8, COLS), f32),
        ],
        (coeffs, boundary, phase) + inputs,
        scalars=3,
        fetched=3,
    )
    tall, thin, spread = ((FIELDS * TALL, COLS), f32), ((THIN * TALL, COLS), f32), ((3, 8 * TALL, COLS), f32)
    off_chip, on_chip, more_own, own_masks = call(
        pack_columns,
        [
            ((COL_MSG + MORE, COLS), f32),
            ((COL_MSG, COLS), f32),
            ((THIN * 2 * DEPTH, COLS), f32),
            ((3, TALL_PAD, COLS), f32),
        ],
        (above, below, masks, heads, tails),
        scratch=[more_msg] * 2,
    )
    pairs = [(i, i + 2 * (i % 2) - 1) for i in range(1, peers_y - 1)]
    off_chip = lax.ppermute(off_chip, "gy", pairs)
    on_chip = lax.ppermute(on_chip, "gy", [(i, i ^ 1) for i in range(peers_y)])
    (main,) = call(
        evolve_main,
        [((FIELDS * ROWS, COLS), f32)],
        (consts, wave, above, below, masks),
        scratch=[spread] + [tall] * 3,
        limit=12,
        flops=20_000_000,
    )
    block = ((FIELDS, ROWS, COLS), jnp.bfloat16)
    evolved, part = call(
        evolve_rest,
        [block, ((peers_y, PART, COLS), f32)],
        (consts, main, own, more_own, own_masks, on_chip, off_chip),
        sent=1,
        scratch=[thin] * 3
        + [spread, ((FIELDS * ROWS, COLS), f32), ((FIELDS, ROWS * COLS), jnp.bfloat16), block],
        limit=12,
        flops=10_000_000,
    )
    total = added(part, "gy")
    total = added(jnp.broadcast_to(total[None], (peers_x,) + total.shape), "gx")
    over = total.reshape(PART, 2, GROUPS, norbit).transpose(2, 1, 0, 3).reshape(2, norbit, norbit)
    return evolved.reshape(state.shape), over


def solution(mesh):
    return jax.shard_map(
        on_device,
        mesh=mesh,
        in_specs=(P(None, None, "gx", "gy"), P("gx", "gy"), P(None, "gx", "gy"), P(), P(), P()),
        out_specs=(P(None, None, "gx", "gy"), P()),
        check_vma=False,
    )
```
